512 devices in a mesh: dp: 16 (over z_lo, x), ctx: 32 (over z_hi, y, core).
Axes of the slice: x: 4, y: 4, z: 16 (z_hi: 4, z_lo: 4; z = z_hi * 4 + z_lo), core: 2. Of those that a mesh axis runs over, the one named last changes fastest.
Arguments:
- tokens: bfloat16 [16, 16384, 512], P('dp', 'ctx'), may hold values from -6 to 6
- cotangent: bfloat16 [16, 16384, 512], P('dp', 'ctx'), may hold values from -6 to 6
- gate_weight: bfloat16 [512, 512], replicated, may hold values from -0.25 to 0.25
- out_weight: bfloat16 [512, 512], replicated, may hold values from -0.25 to 0.25
- left_monarch_matrix: bfloat16 [32, 512, 512], P('ctx'), may hold values from -0.25 to 0.25
- right_factor: bfloat16 [512, 32, 32], P('ctx'), may hold values from -1 to 1
Outputs:
- output: bfloat16 [16, 16384, 512], P('dp', 'ctx')
- grad_tokens: bfloat16 [16, 16384, 512], P('dp', 'ctx')
- grad_gate: float32 [512, 512], P('ctx')
- grad_out: float32 [512, 512], P('ctx')
- grad_left: float32 [32, 512, 512], P('ctx')
- grad_right: float32 [512, 32, 32], P('ctx')
The draws below stay inside these ranges and needn't reach their ends.
All inputs are finite; a program needn't handle non-finite values.
Results may differ from the reference program's by a relative error of at most 0.023.
Values may be sent and summed in bfloat16 or wider, within the bound.
No kernel may reach another device: no remote copies, remote signals or barrier semaphores. Data moves between devices by JAX's collectives and lax.ppermute only.
A program may use at most 64 MiB of HBM per device.

```python
import math
import jax
import jax.numpy as jnp
from jax import lax

MODEL_WIDTH = 512
BLOCK = 512
NB = 32
SEQUENCE_LENGTH = 16384
SEQS = 16


def raised(values, own_key, source, target, blocks, factor):
    def block_of(position):
        return (jnp.arange(values.shape[position]) // (values.shape[position] // blocks)).reshape((-1,) + (1,) * (values.ndim - 1 - position))

    first = jax.random.permutation(own_key, blocks)[block_of(target)]
    other_side = (block_of(target) + blocks // 2) % blocks
    return jnp.where((block_of(source) == first) | (block_of(source) == other_side), factor * values, values)


def level_of(key, shape, cuts, smallest, top_value):
    def one(axis_at, shards_of):
        steps = jax.random.uniform(jax.random.fold_in(jax.random.fold_in(key, 6), axis_at), (shards_of,), jnp.float32, smallest / len(cuts), top_value / len(cuts))
        return jnp.repeat(jnp.exp(steps), shape[axis_at] // shards_of).reshape((-1,) + (1,) * (len(shape) - axis_at - 1))

    loudness = one(*cuts[0])
    for cut in cuts[1:]:
        loudness = loudness * one(*cut)
    return loudness


def normal_values(rng, extent, width, limit, split=(), dtype=jnp.bfloat16):
    entries = width * jax.random.normal(rng, extent, jnp.float32)
    if split:
        entries = entries * level_of(rng, extent, split, -0.22, 0.18)
    return jnp.clip(entries, -limit, limit).astype(dtype)


def gaussian_with(own_key, dims, scale, most, pieces, heavy, kind=jnp.bfloat16):
    drawn = scale * jax.random.normal(own_key, dims, jnp.float32)
    if pieces:
        drawn = drawn * level_of(own_key, dims, pieces, -0.22, 0.18)
    return jnp.clip(raised(drawn, jax.random.fold_in(own_key, 3), *heavy), -most, most).astype(kind)


def setup_inputs(seed: int = 0) -> dict:
    arg_keys = jax.random.split(jax.random.key(seed), 7)
    return {
        "tokens": gaussian_with(arg_keys[0], (SEQS, SEQUENCE_LENGTH, MODEL_WIDTH), 1.0, 6.0, ((0, 16), (1, 32)), (1, 2, 32, 2.75)),
        "cotangent": normal_values(arg_keys[1], (SEQS, SEQUENCE_LENGTH, MODEL_WIDTH), 1.0, 6.0, ((0, 16), (1, 32))),
        "gate_weight": normal_values(arg_keys[2], (MODEL_WIDTH, MODEL_WIDTH), MODEL_WIDTH ** -0.5, 0.25),
        "out_weight": normal_values(arg_keys[3], (MODEL_WIDTH, MODEL_WIDTH), MODEL_WIDTH ** -0.5, 0.25),
        "left_monarch_matrix": normal_values(arg_keys[4], (NB, BLOCK, BLOCK), BLOCK ** -0.5, 0.25, ((0, 32),)),
        "right_factor": normal_values(arg_keys[5], (BLOCK, NB, NB), NB ** -0.5, 1.0, ((0, 32),)),
    }


def silu_parts(gate_pre):
    sigmoid_val = jax.nn.sigmoid(gate_pre)
    return (gate_pre * sigmoid_val, sigmoid_val * (1.0 + gate_pre * (1.0 - sigmoid_val)))

def reference(tokens, cotangent, gate_weight, out_weight, left_monarch_matrix, right_factor):
    weight_scale = 1.0 / math.sqrt(SEQS * SEQUENCE_LENGTH)
    factor_scale = 1.0 / math.sqrt(SEQS * MODEL_WIDTH)
    left_expanded = left_monarch_matrix.astype(jnp.float32)
    right_wide = right_factor.astype(jnp.float32)

    def one_sequence(carry, pair):
        seq_tokens, seq_cotan = pair
        token_blocks = seq_tokens.reshape(NB, BLOCK, MODEL_WIDTH)
        initial_mixing = jnp.einsum('nsg,ngt->nst', left_expanded, token_blocks.astype(jnp.float32)).astype(jnp.bfloat16)
        second_mix = jnp.einsum('pkj,jpd->kpd', right_wide, initial_mixing.astype(jnp.float32)).astype(jnp.bfloat16)
        mixed_rows = second_mix.reshape(SEQUENCE_LENGTH, MODEL_WIDTH).astype(jnp.float32)
        gate_pre = jnp.dot(seq_tokens, gate_weight, preferred_element_type=jnp.float32)
        activated, slope = silu_parts(gate_pre)
        hidden = (mixed_rows * activated).astype(jnp.bfloat16)
        result = jnp.dot(hidden, out_weight, preferred_element_type=jnp.float32).astype(jnp.bfloat16)
        grad_hidden = jnp.dot(seq_cotan, out_weight.T, preferred_element_type=jnp.float32)
        grad_second = (grad_hidden * activated).astype(jnp.bfloat16)
        grad_gate_pre = (grad_hidden * mixed_rows * slope).astype(jnp.bfloat16)
        term_out = jnp.dot(hidden.T, seq_cotan, preferred_element_type=jnp.float32)
        term_gate = jnp.dot(seq_tokens.T, grad_gate_pre, preferred_element_type=jnp.float32)
        grad_blocks = grad_second.reshape(NB, BLOCK, MODEL_WIDTH).astype(jnp.float32)
        initial_gradient = jnp.einsum('pkj,kpd->jpd', right_wide, grad_blocks).astype(jnp.bfloat16)
        term_right = jnp.einsum('kpd,jpd->pkj', grad_blocks, initial_mixing.astype(jnp.float32))
        left_contribution = jnp.einsum('xam,xom->xao', initial_gradient.astype(jnp.float32), token_blocks.astype(jnp.float32))
        after_left_factor = jnp.einsum('hfg,hfe->hge', left_expanded, initial_gradient.astype(jnp.float32)).reshape(SEQUENCE_LENGTH, MODEL_WIDTH)
        through_gate = jnp.dot(grad_gate_pre, gate_weight.T, preferred_element_type=jnp.float32)
        grad_seq = (after_left_factor + through_gate).astype(jnp.bfloat16)
        acc_gate, acc_out, acc_left, acc_right = carry
        carry = (acc_gate + term_gate, acc_out + term_out, acc_left + left_contribution, acc_right + term_right)
        return (carry, (result, grad_seq))
    start = (jnp.zeros((MODEL_WIDTH, MODEL_WIDTH), jnp.float32), jnp.zeros((MODEL_WIDTH, MODEL_WIDTH), jnp.float32), jnp.zeros((NB, BLOCK, BLOCK), jnp.float32), jnp.zeros((BLOCK, NB, NB), jnp.float32))
    totals, stacked = lax.scan(one_sequence, start, (tokens, cotangent))
    acc_gate, acc_out, acc_left, acc_right = totals
    output, grad_tokens = stacked
    return (output, grad_tokens, acc_gate * weight_scale, acc_out * weight_scale, acc_left * factor_scale, acc_right * factor_scale)
```

```python
import math

import jax
import jax.numpy as jnp
from jax import lax
from jax.sharding import Mesh, PartitionSpec as P

DP = ("zl", "x")
CTX = ("zh", "y", "c")
BF = jnp.bfloat16
F32 = jnp.float32


def mm(a, b):
    return jnp.dot(a, b, preferred_element_type=F32)


def mm_t(a, b):
    return lax.dot_general(a, b, (((1,), (1,)), ((), ())), preferred_element_type=F32)


def mm_tl(a, b):
    return lax.dot_general(a, b, (((0,), (0,)), ((), ())), preferred_element_type=F32)


def swap(blocks, axes):
    return lax.all_to_all(blocks, axes, 0, 0, tiled=True)


def per_device(tokens, cotangent, gate_weight, out_weight, left_matrix, right_factor):
    x = tokens[0]
    cot = cotangent[0]
    left = left_matrix[0]
    tok, ch = x.shape
    pos, nb, _ = right_factor.shape
    seqs = lax.axis_size(DP)
    ctx = lax.axis_size(CTX)
    weight_scale = 1.0 / math.sqrt(seqs * ctx * tok)
    factor_scale = 1.0 / math.sqrt(seqs * ch)

    first_mix = mm(left, x).astype(BF)
    first_moved = swap(first_mix.reshape(nb, pos, ch), CTX)

    gate_pre = mm(x, gate_weight)
    grad_hidden = mm_t(cot, out_weight)
    sig = jax.nn.sigmoid(gate_pre)
    activated = gate_pre * sig
    slope = sig * (1.0 + gate_pre * (1.0 - sig))
    grad_second = (grad_hidden * activated).astype(BF)
    grad_moved = swap(grad_second.reshape(nb, pos, ch), CTX)

    same = jnp.eye(pos, dtype=BF)
    wide = (right_factor.transpose(1, 0, 2)[:, :, :, None] * same[None, :, None, :]).reshape(nb * pos, nb * pos)

    first_flat = first_moved.reshape(nb * pos, ch)
    second_moved = mm(wide, first_flat).astype(BF)
    second_mix = swap(second_moved.reshape(nb, pos, ch), CTX)

    first_grad_moved = mm_tl(wide, grad_moved.reshape(nb * pos, ch)).astype(BF)
    initial_gradient = swap(first_grad_moved.reshape(nb, pos, ch), CTX).reshape(tok, ch)

    term_right = jnp.einsum("kpd,jpd->pkj", grad_moved, first_moved, preferred_element_type=F32)

    mixed = second_mix.reshape(tok, ch).astype(F32)
    hidden = (mixed * activated).astype(BF)
    grad_gate_pre = (grad_hidden * mixed * slope).astype(BF)
    result = mm(hidden, out_weight).astype(BF)
    through_gate = mm_t(grad_gate_pre, gate_weight)
    term_gate = mm_tl(x, grad_gate_pre).astype(BF)
    term_out = mm_tl(hidden, cot).astype(BF)

    share = ch // ctx
    zh = lax.axis_size("zh")
    yc = lax.axis_size(("y", "c"))

    def by_yc(term):
        return term.reshape(zh, yc, share, ch).transpose(1, 0, 2, 3)

    terms = jnp.stack([by_yc(term_gate), by_yc(term_out)], 2)
    terms = swap(terms.reshape(yc, zh * 2 * share, ch), ("y", "c"))
    terms = terms.astype(F32).sum(0).astype(BF).reshape(zh, 2 * share, ch)
    terms = swap(terms, "zh").astype(F32).sum(0).astype(BF)
    small = jnp.concatenate([terms, term_right.astype(BF).reshape(-1, ch)], 0)
    small = lax.all_gather(small, DP, axis=0).astype(F32).sum(0)
    sum_gate = small[:share]
    sum_out = small[share : 2 * share]
    sum_right = small[2 * share :].reshape(pos, nb, nb)

    term_left = mm_t(initial_gradient, x).astype(BF)
    part = swap(term_left.reshape(seqs, tok // seqs, tok), DP).astype(F32).sum(0).astype(BF)
    spread = jnp.broadcast_to(part[None], (seqs,) + part.shape)
    sum_left = swap(spread, DP).reshape(1, tok, tok).astype(F32)

    grad_tokens = (mm_tl(left, initial_gradient) + through_gate).astype(BF)

    return (
        result[None],
        grad_tokens[None],
        sum_gate * weight_scale,
        sum_out * weight_scale,
        sum_left * factor_scale,
        sum_right * factor_scale,
    )


def solution(mesh):
    fine = Mesh(mesh.devices.reshape(4, 4, 4, 4, 2), DP + CTX)
    tok = P(DP, CTX, None)
    own = P(CTX, None, None)
    return jax.shard_map(
        per_device,
        mesh=fine,
        in_specs=(tok, tok, P(), P(), own, own),
        out_specs=(tok, tok, P(CTX, None), P(CTX, None), own, own),
        check_vma=False,
    )
```

```python
import math

import jax
import jax.numpy as jnp
from jax import lax
from jax.sharding import Mesh, PartitionSpec as P

DP = ("zl", "x")
CTX = ("zh", "y", "c")
YC = ("y", "c")
BF = jnp.bfloat16
F32 = jnp.float32


def mm(a, b):
    return jnp.dot(a, b, preferred_element_type=F32)


def mm_t(a, b):
    return lax.dot_general(a, b, (((1,), (1,)), ((), ())), preferred_element_type=F32)


def mm_tl(a, b):
    return lax.dot_general(a, b, (((0,), (0,)), ((), ())), preferred_element_type=F32)


def swap(blocks, axes):
    return lax.all_to_all(blocks, axes, 0, 0, tiled=True)


def shift(block, axis, step):
    n = lax.axis_size(axis)
    return lax.ppermute(block, axis, [(i, (i + step) % n) for i in range(n)])


def exchange(blocks, axis, order):
    n = len(blocks)
    got = [blocks[0]] + [None] * (n - 1)
    for m in order:
        got[(n - m) % n] = shift(blocks[m], axis, m)
    return got


def pick(stack, first, n):
    return [lax.dynamic_index_in_dim(stack, (first + m) % n, 0, keepdims=False) for m in range(n)]


def per_device(tokens, cotangent, gate_weight, out_weight, left_matrix, right_factor):
    x = tokens[0]
    cot = cotangent[0]
    left = left_matrix[0]
    tok, ch = x.shape
    pos, nb, _ = right_factor.shape
    seqs = lax.axis_size(DP)
    ctx = lax.axis_size(CTX)
    nz, ny, nx = (lax.axis_size(a) for a in ("zh", "y", "x"))
    yi, ci, xi = (lax.axis_index(a) for a in ("y", "c", "x"))
    weight_scale = 1.0 / math.sqrt(seqs * ctx * tok)
    factor_scale = 1.0 / math.sqrt(seqs * ch)

    first_mix = mm(left, x).astype(BF)
    first_moved = swap(first_mix.reshape(nb, pos, ch), CTX)

    gate_pre = mm(x, gate_weight)
    grad_hidden = mm_t(cot, out_weight)
    sig = jax.nn.sigmoid(gate_pre)
    activated = gate_pre * sig
    slope = sig * (1.0 + gate_pre * (1.0 - sig))
    grad_second = (grad_hidden * activated).astype(BF)

    same = jnp.eye(pos, dtype=BF)
    wide = (right_factor.transpose(1, 0, 2)[:, :, :, None] * same[None, :, None, :]).reshape(nb * pos, nb * pos)

    second_moved = mm(wide, first_moved.reshape(nb * pos, ch)).astype(BF)
    both = jnp.concatenate([second_moved.reshape(nb, pos, ch), grad_second.reshape(nb, pos, ch)], 1)
    both = swap(both, CTX)
    second_mix = both[:, :pos].reshape(tok, ch)
    grad_moved = both[:, pos:]

    first_grad_moved = mm_tl(wide, grad_moved.reshape(nb * pos, ch)).astype(BF)
    initial_gradient = swap(first_grad_moved.reshape(nb, pos, ch), CTX).reshape(tok, ch)

    mixed = second_mix.astype(F32)
    hidden = (mixed * activated).astype(BF)
    grad_gate_pre = (grad_hidden * mixed * slope).astype(BF)
    term_gate = mm_tl(x, grad_gate_pre).astype(BF)
    term_out = mm_tl(hidden, cot).astype(BF)

    share = ch // ctx
    terms = jnp.stack([term_gate, term_out]).reshape(2, nz, ny, 2, share, ch)
    mine = lax.dynamic_index_in_dim(terms, ci, 3, keepdims=False)
    other = lax.dynamic_index_in_dim(terms, 1 - ci, 3, keepdims=False)
    terms = (mine.astype(F32) + shift(other, "c", 1).astype(F32)).astype(BF)
    terms = pick(jnp.moveaxis(terms, 2, 0), yi, ny)
    terms = sum(b.astype(F32) for b in exchange(terms, "y", (2, 1, 3))).astype(BF)
    terms = jnp.moveaxis(terms, 1, 0).reshape(nz, 2 * share, ch)
    terms = swap(terms, "zh").astype(F32).sum(0).astype(BF)

    term_right = jnp.einsum("kpd,jpd->pkj", grad_moved, first_moved, preferred_element_type=F32)
    term_right = term_right.reshape(-1, ch).astype(BF)

    result = mm(hidden, out_weight).astype(BF)
    through_gate = mm_t(grad_gate_pre, gate_weight)

    term_left = mm_t(initial_gradient, x).astype(BF)
    part = pick(term_left.reshape(nx, tok // nx, tok), xi, nx)
    part = sum(b.astype(F32) for b in exchange(part, "x", (2, 1, 3))).astype(BF)

    small = jnp.concatenate([part, terms, term_right], 0)
    small = lax.all_gather(small, "zl", axis=0).astype(F32).sum(0).astype(BF)
    small = swap(jnp.broadcast_to(small[None], (nx,) + small.shape), "x")
    sum_left = small[:, : tok // nx].reshape(1, tok, tok).astype(F32)
    small = small[:, tok // nx :].astype(F32).sum(0)
    sum_gate = small[:share]
    sum_out = small[share : 2 * share]
    sum_right = small[2 * share :].reshape(pos, nb, nb)

    grad_tokens = (mm_tl(left, initial_gradient) + through_gate).astype(BF)

    return (
        result[None],
        grad_tokens[None],
        sum_gate * weight_scale,
        sum_out * weight_scale,
        sum_left * factor_scale,
        sum_right * factor_scale,
    )


def solution(mesh):
    fine = Mesh(mesh.devices.reshape(4, 4, 4, 4, 2), DP + CTX)
    tok = P(DP, CTX, None)
    own = P(CTX, None, None)
    return jax.shard_map(
        per_device,
        mesh=fine,
        in_specs=(tok, tok, P(), P(), own, own),
        out_specs=(tok, tok, P(CTX, None), P(CTX, None), own, own),
        check_vma=False,
    )
```

```python
import functools
import math

import jax
import jax.numpy as jnp
from jax import lax
from jax.experimental import pallas as pl
from jax.experimental.pallas import tpu as pltpu
from jax.sharding import Mesh, PartitionSpec as P

DP = ("zl", "x")
CTX = ("zh", "y", "c")
YC = ("y", "c")
BF = jnp.bfloat16
F32 = jnp.float32


def mm(a, b):
    return jnp.dot(a, b, preferred_element_type=F32)


def mm_t(a, b):
    return lax.dot_general(a, b, (((1,), (1,)), ((), ())), preferred_element_type=F32)


def mm_tl(a, b):
    return lax.dot_general(a, b, (((0,), (0,)), ((), ())), preferred_element_type=F32)


def swap(blocks, axes):
    return lax.all_to_all(blocks, axes, 0, 0, tiled=True)


def shift(block, axis, step):
    n = lax.axis_size(axis)
    return lax.ppermute(block, axis, [(i, (i + step) % n) for i in range(n)])


def exchange(blocks, axis, order):
    n = len(blocks)
    got = [blocks[0]] + [None] * (n - 1)
    for m in order:
        got[(n - m) % n] = shift(blocks[m], axis, m)
    return got


def pick(stack, first, n):
    return [lax.dynamic_index_in_dim(stack, (first + m) % n, 0, keepdims=False) for m in range(n)]


LIMIT = pltpu.CompilerParams(vmem_limit_bytes=56 * 2**20)


def in_vmem(body, out_shape, *args):
    vmem = pl.BlockSpec(memory_space=pltpu.VMEM)
    return pl.pallas_call(
        body,
        out_shape=out_shape,
        in_specs=[vmem] * len(args),
        out_specs=jax.tree.map(lambda _: vmem, out_shape),
        compiler_params=pltpu.CompilerParams(vmem_limit_bytes=32 * 2**20),
    )(*args)


def from_hbm(body, out_shape, *args):
    n = len(args)

    def whole(*refs):
        here, out, there, sems = refs[:n], refs[n:-n - 1], refs[-n - 1 : -1], refs[-1]
        copies = [pltpu.make_async_copy(h, t, sems.at[i]) for i, (h, t) in enumerate(zip(here, there))]
        for copy in copies:
            copy.start()
        body(lambda *which: [copies[i].wait() for i in which], *there, *out)

    return pl.pallas_call(
        whole,
        out_shape=out_shape,
        in_specs=[pl.BlockSpec(memory_space=pltpu.HBM)] * n,
        out_specs=jax.tree.map(lambda _: pl.BlockSpec(memory_space=pltpu.VMEM), out_shape),
        scratch_shapes=[pltpu.VMEM(a.shape, a.dtype) for a in args] + [pltpu.SemaphoreType.DMA((n,))],
        compiler_params=LIMIT,
    )(*args)


def front_body(ready, left, x, gate_weight, cot, out_weight, both):
    nb, two, ch = both.shape
    pos = two // 2
    ready(0, 1)
    both[:, :pos] = mm(left[...], x[...]).astype(BF).reshape(nb, pos, ch)
    ready(2, 3, 4)
    gate_pre = mm(x[...], gate_weight[...])
    grad_hidden = mm_t(cot[...], out_weight[...])
    activated = gate_pre * jax.nn.sigmoid(gate_pre)
    both[:, pos:] = (grad_hidden * activated).astype(BF).reshape(nb, pos, ch)


def middle_body(moved, wide, wide_t, both, right):
    nb, two, ch = both.shape
    pos = two // 2
    rows = nb * pos
    first = moved[:, :pos].reshape(rows, ch)
    grad = moved[:, pos:].reshape(rows, ch)
    both[:, :pos] = mm(wide[...], first).astype(BF).reshape(nb, pos, ch)
    both[:, pos:] = mm(wide_t[...], grad).astype(BF).reshape(nb, pos, ch)
    place = lax.broadcasted_iota(jnp.int32, (rows, rows), 0) % pos
    other = lax.broadcasted_iota(jnp.int32, (rows, rows), 1) % pos
    kept = jnp.where(place == other, mm_t(grad, first), 0.0).astype(BF)
    column = lax.broadcasted_iota(jnp.int32, (rows, 128), 0) // pos
    choose = (column == lax.broadcasted_iota(jnp.int32, (rows, 128), 1)).astype(BF)
    right[...] = mm(kept, choose).astype(BF)


def gate_body(ready, back, activated, sloped, x, cot, hidden, grad_gate_pre, terms):
    tok, ch = x.shape
    yc, nl, nz, part, _ = terms.shape
    pos = back.shape[1] // 2
    ready(0, 1, 2)
    mixed = back[:, :pos].reshape(tok, ch).astype(F32)
    grad_gate_pre[...] = (mixed * sloped[...]).astype(BF)
    hidden[...] = (mixed * activated[...]).astype(BF)
    ready(3, 4)
    for i, term in enumerate((mm_tl(x[...], grad_gate_pre[...]), mm_tl(hidden[...], cot[...]))):
        term = term.reshape(nz, yc, nl // 2, part, ch)
        for half in range(nl // 2):
            for z in range(nz):
                terms[:, i * (nl // 2) + half, z] = term[z, :, half].astype(BF)


def sum_body(parts, total):
    total[...] = parts[...].astype(F32).sum(0).astype(BF)


def pack_body(near, one, two, three, terms, packed):
    part = near[...].astype(F32) + one[...].astype(F32) + two[...].astype(F32) + three[...].astype(F32)
    term = terms[...].astype(F32).sum(0)
    row = jnp.concatenate([part, term], 0).astype(BF)
    packed[...] = jnp.broadcast_to(row[None], packed.shape)


def finish_body(weight_scale, factor_scale, packed, left, gate, out, right):
    seqs, rows, ch = packed.shape
    size = left.shape[0] // seqs
    left[...] = packed[:, :size].astype(F32).reshape(left.shape) * factor_scale
    rest = packed[:, size:].astype(F32)
    right[...] = rest[:, :8, :128] * factor_scale
    share = gate.shape[0]
    terms = rest[:, 8:].reshape(-1, 4, 8, ch).sum(1).reshape(2 * share, ch) * weight_scale
    gate[...] = terms[:share]
    out[...] = terms[share:]


def per_device(tokens, cotangent, gate_weight, out_weight, left_matrix, right_factor):
    x = tokens[0]
    cot = cotangent[0]
    left = left_matrix[0]
    tok, ch = x.shape
    pos, nb, _ = right_factor.shape
    seqs = lax.axis_size(DP)
    ctx = lax.axis_size(CTX)
    nz, nl, nx = (lax.axis_size(a) for a in ("zh", "zl", "x"))
    li, xi = lax.axis_index("zl"), lax.axis_index("x")
    weight_scale = 1.0 / math.sqrt(seqs * ctx * tok)
    factor_scale = 1.0 / math.sqrt(seqs * ch)

    pair = jax.ShapeDtypeStruct((nb, 2 * pos, ch), BF)
    sent = from_hbm(front_body, pair, left, x, gate_weight, cot, out_weight)
    moved = swap(sent, CTX)

    gate_pre = mm(x, gate_weight)
    grad_hidden = mm_t(cot, out_weight)
    sig = jax.nn.sigmoid(gate_pre)
    activated = gate_pre * sig
    slope = sig * (1.0 + gate_pre * (1.0 - sig))

    same = jnp.eye(pos, dtype=BF)[None, :, None, :]
    wide = (right_factor.transpose(1, 0, 2)[:, :, :, None] * same).reshape(nb * pos, nb * pos)
    wide_t = (right_factor.transpose(2, 0, 1)[:, :, :, None] * same).reshape(nb * pos, nb * pos)
    right_shape = jax.ShapeDtypeStruct((nb * pos, 128), BF)
    sent, term_right = in_vmem(middle_body, (pair, right_shape), moved, wide, wide_t)
    back = swap(sent, CTX)

    term_right = term_right[:, :nb].reshape(nb, pos, nb).transpose(1, 0, 2).reshape(nl, nx, -1, 128)
    term_right = jnp.pad(term_right, ((0, 0), (0, 0), (0, 0), (0, ch - 128)))

    share = ch // ctx
    yc = lax.axis_size(YC)
    token_pair = jax.ShapeDtypeStruct((tok, ch), BF)
    gated = (token_pair, token_pair, jax.ShapeDtypeStruct((yc, nl, nz, 2 * share // nl, ch), BF))
    hidden, grad_gate_pre, terms = from_hbm(gate_body, gated, back, activated, grad_hidden * slope, x, cot)
    initial_gradient = back[:, pos:].reshape(tok, ch)

    terms = swap(terms.reshape(yc, nz * 2 * share, ch), YC)
    terms = in_vmem(sum_body, jax.ShapeDtypeStruct(terms.shape[1:], BF), terms)
    terms = swap(terms.reshape(nl * nz, -1, ch), ("zl", "zh"))

    result = mm(hidden, out_weight).astype(BF)
    through_gate = mm_t(grad_gate_pre, gate_weight)

    term_left = mm_t(initial_gradient, x).astype(BF)
    part = jnp.concatenate([term_left.reshape(nl, nx, -1, tok), term_right], 2)
    part = jnp.moveaxis(part, 1, 0)
    part = sum(b.astype(F32) for b in exchange(pick(part, xi, nx), "x", (2, 1, 3))).astype(BF)
    near, one, two, three = exchange(pick(part, li, nl), "zl", (2, 1, 3))
    packed = jax.ShapeDtypeStruct((seqs, near.shape[0] + terms.shape[1], ch), BF)
    packed = swap(in_vmem(pack_body, packed, near, one, two, three, terms), DP)
    finished = (
        jax.ShapeDtypeStruct((tok, tok), F32),
        jax.ShapeDtypeStruct((share, ch), F32),
        jax.ShapeDtypeStruct((share, ch), F32),
        jax.ShapeDtypeStruct((seqs, 8, 128), F32),
    )
    finish = functools.partial(finish_body, weight_scale, factor_scale)
    sum_left, sum_gate, sum_out, sum_right = in_vmem(finish, finished, packed)

    grad_tokens = (mm_tl(left, initial_gradient) + through_gate).astype(BF)

    return (
        result[None],
        grad_tokens[None],
        sum_gate,
        sum_out,
        sum_left[None],
        sum_right.reshape(pos, nb, nb),
    )


def solution(mesh):
    fine = Mesh(mesh.devices.reshape(4, 4, 4, 4, 2), DP + CTX)
    tok = P(DP, CTX, None)
    own = P(CTX, None, None)
    return jax.shard_map(
        per_device,
        mesh=fine,
        in_specs=(tok, tok, P(), P(), own, own),
        out_specs=(tok, tok, P(CTX, None), P(CTX, None), own, own),
        check_vma=False,
    )
```

```python
import functools
import math

import jax
import jax.numpy as jnp
from jax import lax
from jax.experimental import pallas as pl
from jax.experimental.pallas import tpu as pltpu
from jax.sharding import Mesh, PartitionSpec as P

DP = ("zl", "x")
CTX = ("zh", "y", "c")
YC = ("y", "c")
BF = jnp.bfloat16
F32 = jnp.float32


def mm(a, b):
    return jnp.dot(a, b, preferred_element_type=F32)


def mm_t(a, b):
    return lax.dot_general(a, b, (((1,), (1,)), ((), ())), preferred_element_type=F32)


def mm_tl(a, b):
    return lax.dot_general(a, b, (((0,), (0,)), ((), ())), preferred_element_type=F32)


def swap(blocks, axes):
    return lax.all_to_all(blocks, axes, 0, 0, tiled=True)


def shift(block, axis, step):
    n = lax.axis_size(axis)
    return lax.ppermute(block, axis, [(i, (i + step) % n) for i in range(n)])


def exchange(blocks, axis, order):
    n = len(blocks)
    got = [blocks[0]] + [None] * (n - 1)
    for m in order:
        got[(n - m) % n] = shift(blocks[m], axis, m)
    return got


def pick(stack, first, n):
    return [lax.dynamic_index_in_dim(stack, (first + m) % n, 0, keepdims=False) for m in range(n)]


LIMIT = pltpu.CompilerParams(vmem_limit_bytes=56 * 2**20)


def in_vmem(body, out_shape, *args):
    vmem = pl.BlockSpec(memory_space=pltpu.VMEM)
    return pl.pallas_call(
        body,
        out_shape=out_shape,
        in_specs=[vmem] * len(args),
        out_specs=jax.tree.map(lambda _: vmem, out_shape),
        compiler_params=pltpu.CompilerParams(vmem_limit_bytes=32 * 2**20),
    )(*args)


def from_hbm(body, out_shape, *args):
    n = len(args)

    def whole(*refs):
        here, out, there, sems = refs[:n], refs[n:-n - 1], refs[-n - 1 : -1], refs[-1]
        copies = [pltpu.make_async_copy(h, t, sems.at[i]) for i, (h, t) in enumerate(zip(here, there))]
        for copy in copies:
            copy.start()
        body(lambda *which: [copies[i].wait() for i in which], *there, *out)

    return pl.pallas_call(
        whole,
        out_shape=out_shape,
        in_specs=[pl.BlockSpec(memory_space=pltpu.HBM)] * n,
        out_specs=jax.tree.map(lambda _: pl.BlockSpec(memory_space=pltpu.VMEM), out_shape),
        scratch_shapes=[pltpu.VMEM(a.shape, a.dtype) for a in args] + [pltpu.SemaphoreType.DMA((n,))],
        compiler_params=LIMIT,
    )(*args)


def front_body(ready, left, x, gate_weight, cot, out_weight, both):
    nb, two, ch = both.shape
    pos = two // 2
    ready(0, 1)
    both[:, :pos] = mm(left[...], x[...]).astype(BF).reshape(nb, pos, ch)
    ready(2, 3, 4)
    gate_pre = mm(x[...], gate_weight[...])
    grad_hidden = mm_t(cot[...], out_weight[...])
    activated = gate_pre * jax.nn.sigmoid(gate_pre)
    both[:, pos:] = (grad_hidden * activated).astype(BF).reshape(nb, pos, ch)


def middle_body(moved, wide, wide_t, both, right):
    nb, two, ch = both.shape
    pos = two // 2
    rows = nb * pos
    first = moved[:, :pos].reshape(rows, ch)
    grad = moved[:, pos:].reshape(rows, ch)
    both[:, :pos] = mm(wide[...], first).astype(BF).reshape(nb, pos, ch)
    both[:, pos:] = mm(wide_t[...], grad).astype(BF).reshape(nb, pos, ch)
    place = lax.broadcasted_iota(jnp.int32, (rows, rows), 0) % pos
    other = lax.broadcasted_iota(jnp.int32, (rows, rows), 1) % pos
    kept = jnp.where(place == other, mm_t(grad, first), 0.0).astype(BF)
    column = lax.broadcasted_iota(jnp.int32, (rows, 128), 0) // pos
    choose = (column == lax.broadcasted_iota(jnp.int32, (rows, 128), 1)).astype(BF)
    right[...] = mm(kept, choose).astype(BF)


def sum_body(parts, total):
    total[...] = parts[...].astype(F32).sum(0).astype(BF)


def pack_body(near, one, two, three, terms, packed):
    part = near[...].astype(F32) + one[...].astype(F32) + two[...].astype(F32) + three[...].astype(F32)
    term = terms[...].astype(F32).sum(0)
    row = jnp.concatenate([part, term], 0).astype(BF)
    packed[...] = jnp.broadcast_to(row[None], packed.shape)


def finish_body(weight_scale, factor_scale, packed, left, gate, out, right):
    seqs, rows, ch = packed.shape
    size = left.shape[0] // seqs
    left[...] = packed[:, :size].astype(F32).reshape(left.shape) * factor_scale
    rest = packed[:, size:].astype(F32)
    for g in range(right.shape[1] // 8):
        right[:, 8 * g : 8 * (g + 1)] = rest[:, :8, 128 * g : 128 * g + right.shape[2]] * factor_scale
    share = gate.shape[0]
    terms = rest[:, 8:].reshape(-1, 4, 8, ch).sum(1).reshape(2 * share, ch) * weight_scale
    gate[...] = terms[:share]
    out[...] = terms[share:]


def per_device(tokens, cotangent, gate_weight, out_weight, left_matrix, right_factor):
    x = tokens[0]
    cot = cotangent[0]
    left = left_matrix[0]
    tok, ch = x.shape
    pos, nb, _ = right_factor.shape
    seqs = lax.axis_size(DP)
    ctx = lax.axis_size(CTX)
    nz, nl, nx = (lax.axis_size(a) for a in ("zh", "zl", "x"))
    li, xi = lax.axis_index("zl"), lax.axis_index("x")
    weight_scale = 1.0 / math.sqrt(seqs * ctx * tok)
    factor_scale = 1.0 / math.sqrt(seqs * ch)

    pair = jax.ShapeDtypeStruct((nb, 2 * pos, ch), BF)
    sent = from_hbm(front_body, pair, left, x, gate_weight, cot, out_weight)
    moved = swap(sent, CTX)

    gate_pre = mm(x, gate_weight)
    grad_hidden = mm_t(cot, out_weight)
    sig = jax.nn.sigmoid(gate_pre)
    activated = gate_pre * sig
    slope = sig * (1.0 + gate_pre * (1.0 - sig))

    same = jnp.eye(pos, dtype=BF)[None, :, None, :]
    wide = (right_factor.transpose(1, 0, 2)[:, :, :, None] * same).reshape(nb * pos, nb * pos)
    wide_t = (right_factor.transpose(2, 0, 1)[:, :, :, None] * same).reshape(nb * pos, nb * pos)
    right_shape = jax.ShapeDtypeStruct((nb * pos, 128), BF)
    sent, term_right = in_vmem(middle_body, (pair, right_shape), moved, wide, wide_t)
    back = swap(sent, CTX)

    term_right = term_right.reshape(nb // 8, 8, pos, 128).transpose(2, 1, 0, 3).reshape(nl, nx, 8, ch)

    share = ch // ctx
    yc = lax.axis_size(YC)
    mixed = back[:, :pos].reshape(tok, ch).astype(F32)
    hidden = (mixed * activated).astype(BF)
    grad_gate_pre = (grad_hidden * mixed * slope).astype(BF)

    def by_yc(term):
        return term.astype(BF).reshape(nz, yc, nl // 2, -1, ch).transpose(1, 2, 0, 3, 4)

    terms = jnp.concatenate([by_yc(mm_tl(x, grad_gate_pre)), by_yc(mm_tl(hidden, cot))], 1)
    initial_gradient = back[:, pos:].reshape(tok, ch)

    terms = swap(terms.reshape(yc, nz * 2 * share, ch), YC)
    terms = in_vmem(sum_body, jax.ShapeDtypeStruct(terms.shape[1:], BF), terms)
    terms = swap(terms.reshape(nl * nz, -1, ch), ("zl", "zh"))

    result = mm(hidden, out_weight).astype(BF)
    through_gate = mm_t(grad_gate_pre, gate_weight)

    term_left = mm_t(initial_gradient, x).astype(BF)
    part = jnp.concatenate([term_left.reshape(nl, nx, -1, tok), term_right], 2)
    part = jnp.moveaxis(part, 1, 0)
    part = sum(b.astype(F32) for b in exchange(pick(part, xi, nx), "x", (2, 1, 3))).astype(BF)
    near, one, two, three = exchange(pick(part, li, nl), "zl", (2, 1, 3))
    packed = jax.ShapeDtypeStruct((seqs, near.shape[0] + terms.shape[1], ch), BF)
    packed = swap(in_vmem(pack_body, packed, near, one, two, three, terms), DP)
    finished = (
        jax.ShapeDtypeStruct((tok, tok), F32),
        jax.ShapeDtypeStruct((share, ch), F32),
        jax.ShapeDtypeStruct((share, ch), F32),
        jax.ShapeDtypeStruct((pos, nb, nb), F32),
    )
    finish = functools.partial(finish_body, weight_scale, factor_scale)
    sum_left, sum_gate, sum_out, sum_right = in_vmem(finish, finished, packed)

    grad_tokens = (mm_tl(left, initial_gradient) + through_gate).astype(BF)

    return (
        result[None],
        grad_tokens[None],
        sum_gate,
        sum_out,
        sum_left[None],
        sum_right,
    )


def solution(mesh):
    fine = Mesh(mesh.devices.reshape(4, 4, 4, 4, 2), DP + CTX)
    tok = P(DP, CTX, None)
    own = P(CTX, None, None)
    return jax.shard_map(
        per_device,
        mesh=fine,
        in_specs=(tok, tok, P(), P(), own, own),
        out_specs=(tok, tok, P(CTX, None), P(CTX, None), own, own),
        check_vma=False,
    )
```

```python
import functools
import math

import jax
import jax.numpy as jnp
from jax import lax
from jax.experimental import pallas as pl
from jax.experimental.pallas import tpu as pltpu
from jax.sharding import Mesh, PartitionSpec as P

DP = ("zl", "x")
CTX = ("zh", "y", "c")
YC = ("y", "c")
BF = jnp.bfloat16
F32 = jnp.float32


def mm(a, b):
    return jnp.dot(a, b, preferred_element_type=F32)


def mm_t(a, b):
    return lax.dot_general(a, b, (((1,), (1,)), ((), ())), preferred_element_type=F32)


def mm_tl(a, b):
    return lax.dot_general(a, b, (((0,), (0,)), ((), ())), preferred_element_type=F32)


def swap(blocks, axes):
    return lax.all_to_all(blocks, axes, 0, 0, tiled=True)


def shift(block, axis, step):
    n = lax.axis_size(axis)
    return lax.ppermute(block, axis, [(i, (i + step) % n) for i in range(n)])


def exchange(blocks, axis, order):
    n = len(blocks)
    got = [blocks[0]] + [None] * (n - 1)
    for m in order:
        got[(n - m) % n] = shift(blocks[m], axis, m)
    return got


def pick(stack, first, n):
    return [lax.dynamic_index_in_dim(stack, (first + m) % n, 0, keepdims=False) for m in range(n)]


LIMIT = pltpu.CompilerParams(vmem_limit_bytes=56 * 2**20)


def in_vmem(body, out_shape, *args):
    vmem = pl.BlockSpec(memory_space=pltpu.VMEM)
    return pl.pallas_call(
        body,
        out_shape=out_shape,
        in_specs=[vmem] * len(args),
        out_specs=jax.tree.map(lambda _: vmem, out_shape),
        compiler_params=pltpu.CompilerParams(vmem_limit_bytes=32 * 2**20),
    )(*args)


def from_hbm(body, out_shape, *args):
    n = len(args)

    def whole(*refs):
        here, out, there, sems = refs[:n], refs[n:-n - 1], refs[-n - 1 : -1], refs[-1]
        copies = [pltpu.make_async_copy(h, t, sems.at[i]) for i, (h, t) in enumerate(zip(here, there))]
        for copy in copies:
            copy.start()
        body(lambda *which: [copies[i].wait() for i in which], *there, *out)

    return pl.pallas_call(
        whole,
        out_shape=out_shape,
        in_specs=[pl.BlockSpec(memory_space=pltpu.HBM)] * n,
        out_specs=jax.tree.map(lambda _: pl.BlockSpec(memory_space=pltpu.VMEM), out_shape),
        scratch_shapes=[pltpu.VMEM(a.shape, a.dtype) for a in args] + [pltpu.SemaphoreType.DMA((n,))],
        compiler_params=LIMIT,
    )(*args)


def front_body(ready, left, x, gate_weight, cot, out_weight, both):
    nb, two, ch = both.shape
    pos = two // 2
    ready(0, 1)
    both[:, :pos] = mm(left[...], x[...]).astype(BF).reshape(nb, pos, ch)
    ready(2, 3, 4)
    gate_pre = mm(x[...], gate_weight[...])
    grad_hidden = mm_t(cot[...], out_weight[...])
    activated = gate_pre * jax.nn.sigmoid(gate_pre)
    both[:, pos:] = (grad_hidden * activated).astype(BF).reshape(nb, pos, ch)


def middle_body(moved, wide, wide_t, both, right):
    nb, two, ch = both.shape
    pos = two // 2
    rows = nb * pos
    first = moved[:, :pos].reshape(rows, ch)
    grad = moved[:, pos:].reshape(rows, ch)
    both[:, :pos] = mm(wide[...], first).astype(BF).reshape(nb, pos, ch)
    both[:, pos:] = mm(wide_t[...], grad).astype(BF).reshape(nb, pos, ch)
    place = lax.broadcasted_iota(jnp.int32, (rows, rows), 0) % pos
    other = lax.broadcasted_iota(jnp.int32, (rows, rows), 1) % pos
    kept = jnp.where(place == other, mm_t(grad, first), 0.0).astype(BF)
    column = lax.broadcasted_iota(jnp.int32, (rows, 128), 0) // pos
    choose = (column == lax.broadcasted_iota(jnp.int32, (rows, 128), 1)).astype(BF)
    right[...] = mm(kept, choose).astype(BF)


def sum_body(parts, total):
    total[...] = parts[...].astype(F32).sum(0).astype(BF)


def pack_body(near, one, two, three, terms, packed):
    part = near[...].astype(F32) + one[...].astype(F32) + two[...].astype(F32) + three[...].astype(F32)
    term = terms[...].astype(F32).sum(0)
    row = jnp.concatenate([part, term], 0).astype(BF)
    packed[...] = jnp.broadcast_to(row[None], packed.shape)


def finish_body(weight_scale, factor_scale, packed, left, gate, out, right):
    seqs, rows, ch = packed.shape
    size = left.shape[0] // seqs
    left[...] = packed[:, :size].astype(F32).reshape(left.shape) * factor_scale
    rest = packed[:, size:].astype(F32)
    for g in range(right.shape[1] // 8):
        right[:, 8 * g : 8 * (g + 1)] = rest[:, :8, 128 * g : 128 * g + right.shape[2]] * factor_scale
    share = gate.shape[0]
    terms = rest[:, 8:].reshape(-1, 4, 8, ch).sum(1).reshape(2 * share, ch) * weight_scale
    gate[...] = terms[:share]
    out[...] = terms[share:]


def per_device(tokens, cotangent, gate_weight, out_weight, left_matrix, right_factor):
    x = tokens[0]
    cot = cotangent[0]
    left = left_matrix[0]
    tok, ch = x.shape
    pos, nb, _ = right_factor.shape
    seqs = lax.axis_size(DP)
    ctx = lax.axis_size(CTX)
    nz, nl, nx = (lax.axis_size(a) for a in ("zh", "zl", "x"))
    li, xi = lax.axis_index("zl"), lax.axis_index("x")
    weight_scale = 1.0 / math.sqrt(seqs * ctx * tok)
    factor_scale = 1.0 / math.sqrt(seqs * ch)

    pair = jax.ShapeDtypeStruct((nb, 2 * pos, ch), BF)
    sent = from_hbm(front_body, pair, left, x, gate_weight, cot, out_weight)
    moved = swap(sent, CTX)

    gate_pre = mm(x, gate_weight)
    grad_hidden = mm_t(cot, out_weight)
    sig = jax.nn.sigmoid(gate_pre)
    activated = gate_pre * sig
    slope = sig * (1.0 + gate_pre * (1.0 - sig))

    same = jnp.eye(pos, dtype=BF)[None, :, None, :]
    wide = (right_factor.transpose(1, 0, 2)[:, :, :, None] * same).reshape(nb * pos, nb * pos)
    wide_t = (right_factor.transpose(2, 0, 1)[:, :, :, None] * same).reshape(nb * pos, nb * pos)
    sloped = grad_hidden * slope
    moved, activated, sloped = lax.optimization_barrier((moved, activated, sloped))
    right_shape = jax.ShapeDtypeStruct((nb * pos, 128), BF)
    sent, term_right = in_vmem(middle_body, (pair, right_shape), moved, wide, wide_t)
    back = swap(sent, CTX)

    term_right = term_right.reshape(nb // 8, 8, pos, 128).transpose(2, 1, 0, 3).reshape(nl, nx, 8, ch)

    share = ch // ctx
    yc = lax.axis_size(YC)
    mixed = back[:, :pos].reshape(tok, ch).astype(F32)
    hidden = (mixed * activated).astype(BF)
    grad_gate_pre = (mixed * sloped).astype(BF)

    def by_yc(term):
        return term.astype(BF).reshape(nz, yc, nl // 2, -1, ch).transpose(1, 2, 0, 3, 4)

    terms = jnp.concatenate([by_yc(mm_tl(x, grad_gate_pre)), by_yc(mm_tl(hidden, cot))], 1)
    initial_gradient = back[:, pos:].reshape(tok, ch)

    terms = swap(terms.reshape(yc, nz * 2 * share, ch), YC)
    terms = in_vmem(sum_body, jax.ShapeDtypeStruct(terms.shape[1:], BF), terms)
    terms = swap(terms.reshape(nl * nz, -1, ch), ("zl", "zh"))

    result = mm(hidden, out_weight).astype(BF)
    through_gate = mm_t(grad_gate_pre, gate_weight)

    term_left = mm_t(initial_gradient, x).astype(BF)
    part = jnp.concatenate([term_left.reshape(nl, nx, -1, tok), term_right], 2)
    part = jnp.moveaxis(part, 1, 0)
    part = sum(b.astype(F32) for b in exchange(pick(part, xi, nx), "x", (2, 1, 3))).astype(BF)
    near, one, two, three = exchange(pick(part, li, nl), "zl", (2, 1, 3))
    packed = jax.ShapeDtypeStruct((seqs, near.shape[0] + terms.shape[1], ch), BF)
    packed = swap(in_vmem(pack_body, packed, near, one, two, three, terms), DP)
    finished = (
        jax.ShapeDtypeStruct((tok, tok), F32),
        jax.ShapeDtypeStruct((share, ch), F32),
        jax.ShapeDtypeStruct((share, ch), F32),
        jax.ShapeDtypeStruct((pos, nb, nb), F32),
    )
    finish = functools.partial(finish_body, weight_scale, factor_scale)
    sum_left, sum_gate, sum_out, sum_right = in_vmem(finish, finished, packed)

    grad_tokens = (mm_tl(left, initial_gradient) + through_gate).astype(BF)

    return (
        result[None],
        grad_tokens[None],
        sum_gate,
        sum_out,
        sum_left[None],
        sum_right,
    )


def solution(mesh):
    fine = Mesh(mesh.devices.reshape(4, 4, 4, 4, 2), DP + CTX)
    tok = P(DP, CTX, None)
    own = P(CTX, None, None)
    return jax.shard_map(
        per_device,
        mesh=fine,
        in_specs=(tok, tok, P(), P(), own, own),
        out_specs=(tok, tok, P(CTX, None), P(CTX, None), own, own),
        check_vma=False,
    )
```

```python
import functools
import math

import jax
import jax.numpy as jnp
from jax import lax
from jax.experimental import pallas as pl
from jax.experimental.pallas import tpu as pltpu
from jax.sharding import Mesh, PartitionSpec as P

DP = ("zl", "x")
CTX = ("zh", "y", "c")
YC = ("y", "c")
BF = jnp.bfloat16
F32 = jnp.float32


def mm(a, b):
    return jnp.dot(a, b, preferred_element_type=F32)


def mm_t(a, b):
    return lax.dot_general(a, b, (((1,), (1,)), ((), ())), preferred_element_type=F32)


def mm_tl(a, b):
    return lax.dot_general(a, b, (((0,), (0,)), ((), ())), preferred_element_type=F32)


def swap(blocks, axes):
    return lax.all_to_all(blocks, axes, 0, 0, tiled=True)


def shift(block, axis, step):
    n = lax.axis_size(axis)
    return lax.ppermute(block, axis, [(i, (i + step) % n) for i in range(n)])


def exchange(blocks, axis, order):
    n = len(blocks)
    got = [blocks[0]] + [None] * (n - 1)
    for m in order:
        got[(n - m) % n] = shift(blocks[m], axis, m)
    return got


def pick(stack, first, n):
    return [lax.dynamic_index_in_dim(stack, (first + m) % n, 0, keepdims=False) for m in range(n)]


LIMIT = pltpu.CompilerParams(vmem_limit_bytes=56 * 2**20)


def in_vmem(body, out_shape, *args):
    vmem = pl.BlockSpec(memory_space=pltpu.VMEM)
    return pl.pallas_call(
        body,
        out_shape=out_shape,
        in_specs=[vmem] * len(args),
        out_specs=jax.tree.map(lambda _: vmem, out_shape),
        compiler_params=pltpu.CompilerParams(vmem_limit_bytes=32 * 2**20),
    )(*args)


def from_hbm(body, out_shape, *args):
    n = len(args)

    def whole(*refs):
        here, out, there, sems = refs[:n], refs[n:-n - 1], refs[-n - 1 : -1], refs[-1]
        copies = [pltpu.make_async_copy(h, t, sems.at[i]) for i, (h, t) in enumerate(zip(here, there))]
        for copy in copies:
            copy.start()
        body(lambda *which: [copies[i].wait() for i in which], *there, *out)

    return pl.pallas_call(
        whole,
        out_shape=out_shape,
        in_specs=[pl.BlockSpec(memory_space=pltpu.HBM)] * n,
        out_specs=jax.tree.map(lambda _: pl.BlockSpec(memory_space=pltpu.VMEM), out_shape),
        scratch_shapes=[pltpu.VMEM(a.shape, a.dtype) for a in args] + [pltpu.SemaphoreType.DMA((n,))],
        compiler_params=LIMIT,
    )(*args)


def front_body(ready, left, x, gate_weight, cot, out_weight, both):
    nb, two, ch = both.shape
    pos = two // 2
    ready(0, 1)
    both[:, :pos] = mm(left[...], x[...]).astype(BF).reshape(nb, pos, ch)
    ready(2, 3, 4)
    gate_pre = mm(x[...], gate_weight[...])
    grad_hidden = mm_t(cot[...], out_weight[...])
    activated = gate_pre * jax.nn.sigmoid(gate_pre)
    both[:, pos:] = (grad_hidden * activated).astype(BF).reshape(nb, pos, ch)


def middle_body(moved, wide, wide_t, both, right):
    nb, two, ch = both.shape
    pos = two // 2
    rows = nb * pos
    first = moved[:, :pos].reshape(rows, ch)
    grad = moved[:, pos:].reshape(rows, ch)
    both[:, :pos] = mm(wide[...], first).astype(BF).reshape(nb, pos, ch)
    both[:, pos:] = mm(wide_t[...], grad).astype(BF).reshape(nb, pos, ch)
    place = lax.broadcasted_iota(jnp.int32, (rows, rows), 0) % pos
    other = lax.broadcasted_iota(jnp.int32, (rows, rows), 1) % pos
    kept = jnp.where(place == other, mm_t(grad, first), 0.0).astype(BF)
    column = lax.broadcasted_iota(jnp.int32, (rows, 128), 0) // pos
    choose = (column == lax.broadcasted_iota(jnp.int32, (rows, 128), 1)).astype(BF)
    right[...] = mm(kept, choose).astype(BF)


def terms_body(x, grad_gate_pre, hidden, cot, terms):
    yc, nl, nz, part, ch = terms.shape
    for i, term in enumerate((mm_tl(x[...], grad_gate_pre[...]), mm_tl(hidden[...], cot[...]))):
        term = term.reshape(nz, yc, nl // 2, part, ch)
        for half in range(nl // 2):
            for z in range(nz):
                terms[:, i * (nl // 2) + half, z] = term[z, :, half].astype(BF)


def sum_body(parts, total):
    total[...] = parts[...].astype(F32).sum(0).astype(BF)


def pack_body(near, one, two, three, terms, packed):
    part = near[...].astype(F32) + one[...].astype(F32) + two[...].astype(F32) + three[...].astype(F32)
    term = terms[...].astype(F32).sum(0)
    row = jnp.concatenate([part, term], 0).astype(BF)
    packed[...] = jnp.broadcast_to(row[None], packed.shape)


def finish_body(weight_scale, factor_scale, packed, left, gate, out, right):
    seqs, rows, ch = packed.shape
    size = left.shape[0] // seqs
    left[...] = packed[:, :size].astype(F32).reshape(left.shape) * factor_scale
    rest = packed[:, size:].astype(F32)
    for g in range(right.shape[1] // 8):
        right[:, 8 * g : 8 * (g + 1)] = rest[:, :8, 128 * g : 128 * g + right.shape[2]] * factor_scale
    share = gate.shape[0]
    terms = rest[:, 8:].reshape(-1, 4, 8, ch).sum(1).reshape(2 * share, ch) * weight_scale
    gate[...] = terms[:share]
    out[...] = terms[share:]


def per_device(tokens, cotangent, gate_weight, out_weight, left_matrix, right_factor):
    x = tokens[0]
    cot = cotangent[0]
    left = left_matrix[0]
    tok, ch = x.shape
    pos, nb, _ = right_factor.shape
    seqs = lax.axis_size(DP)
    ctx = lax.axis_size(CTX)
    nz, nl, nx = (lax.axis_size(a) for a in ("zh", "zl", "x"))
    li, xi = lax.axis_index("zl"), lax.axis_index("x")
    weight_scale = 1.0 / math.sqrt(seqs * ctx * tok)
    factor_scale = 1.0 / math.sqrt(seqs * ch)

    pair = jax.ShapeDtypeStruct((nb, 2 * pos, ch), BF)
    sent = from_hbm(front_body, pair, left, x, gate_weight, cot, out_weight)
    moved = swap(sent, CTX)

    gate_pre = mm(x, gate_weight)
    grad_hidden = mm_t(cot, out_weight)
    sig = jax.nn.sigmoid(gate_pre)
    activated = gate_pre * sig
    slope = sig * (1.0 + gate_pre * (1.0 - sig))

    same = jnp.eye(pos, dtype=BF)[None, :, None, :]
    wide = (right_factor.transpose(1, 0, 2)[:, :, :, None] * same).reshape(nb * pos, nb * pos)
    wide_t = (right_factor.transpose(2, 0, 1)[:, :, :, None] * same).reshape(nb * pos, nb * pos)
    sloped = grad_hidden * slope
    moved, activated, sloped = lax.optimization_barrier((moved, activated, sloped))
    right_shape = jax.ShapeDtypeStruct((nb * pos, 128), BF)
    sent, term_right = in_vmem(middle_body, (pair, right_shape), moved, wide, wide_t)
    back = swap(sent, CTX)

    term_right = term_right.reshape(nb // 8, 8, pos, 128).transpose(2, 1, 0, 3).reshape(nl, nx, 8, ch)

    share = ch // ctx
    yc = lax.axis_size(YC)
    mixed = back[:, :pos].reshape(tok, ch).astype(F32)
    hidden = (mixed * activated).astype(BF)
    grad_gate_pre = (mixed * sloped).astype(BF)

    laid = jax.ShapeDtypeStruct((yc, nl, nz, 2 * share // nl, ch), BF)
    terms = in_vmem(terms_body, laid, x, grad_gate_pre, hidden, cot)
    initial_gradient = back[:, pos:].reshape(tok, ch)

    terms = swap(terms.reshape(yc, nz * 2 * share, ch), YC)
    terms = in_vmem(sum_body, jax.ShapeDtypeStruct(terms.shape[1:], BF), terms)
    terms = swap(terms.reshape(nl * nz, -1, ch), ("zl", "zh"))

    result = mm(hidden, out_weight).astype(BF)
    through_gate = mm_t(grad_gate_pre, gate_weight)

    term_left = mm_t(initial_gradient, x).astype(BF)
    part = jnp.concatenate([term_left.reshape(nl, nx, -1, tok), term_right], 2)
    part = jnp.moveaxis(part, 1, 0)
    part = sum(b.astype(F32) for b in exchange(pick(part, xi, nx), "x", (2, 1, 3))).astype(BF)
    near, one, two, three = exchange(pick(part, li, nl), "zl", (2, 1, 3))
    packed = jax.ShapeDtypeStruct((seqs, near.shape[0] + terms.shape[1], ch), BF)
    packed = swap(in_vmem(pack_body, packed, near, one, two, three, terms), DP)
    finished = (
        jax.ShapeDtypeStruct((tok, tok), F32),
        jax.ShapeDtypeStruct((share, ch), F32),
        jax.ShapeDtypeStruct((share, ch), F32),
        jax.ShapeDtypeStruct((pos, nb, nb), F32),
    )
    finish = functools.partial(finish_body, weight_scale, factor_scale)
    sum_left, sum_gate, sum_out, sum_right = in_vmem(finish, finished, packed)

    grad_tokens = (mm_tl(left, initial_gradient) + through_gate).astype(BF)

    return (
        result[None],
        grad_tokens[None],
        sum_gate,
        sum_out,
        sum_left[None],
        sum_right,
    )


def solution(mesh):
    fine = Mesh(mesh.devices.reshape(4, 4, 4, 4, 2), DP + CTX)
    tok = P(DP, CTX, None)
    own = P(CTX, None, None)
    return jax.shard_map(
        per_device,
        mesh=fine,
        in_specs=(tok, tok, P(), P(), own, own),
        out_specs=(tok, tok, P(CTX, None), P(CTX, None), own, own),
        check_vma=False,
    )
```
